512 devices in a mesh: dp: 64 (over z, x, core), mp: 8 (over y).
Axes of the slice: x: 4, y: 8, z: 8, core: 2. Of those that a mesh axis runs over, the one named last changes fastest.
Arguments:
- activations: bfloat16 [8192, 4096], P('dp', 'mp'), may hold values from -6 to 6
- cotangent: bfloat16 [8192, 14336], P(('dp', 'mp')), may hold values from -0.0625 to 0.0625
- master: float32 [14336, 4096], P('dp', 'mp'), may hold values from -6 to 6
- first_moment: float32 [14336, 4096], P('dp', 'mp'), may hold values from -6 to 6
- second_moment: float32 [14336, 4096], P('dp', 'mp'), may hold values from 0.25 to 4
- new_owner: int32 [7168], P('dp'), may hold values from 0 to 63, as said below
- new_slot: int32 [7168], P('dp'), may hold values from 0 to 113, as said below
Outputs:
- new_master: float32 [14592, 4096], P('dp', 'mp')
- new_moment1: float32 [14592, 4096], P('dp', 'mp')
- new_moment2: float32 [14592, 4096], P('dp', 'mp')
- new_weights: bfloat16 [14592, 4096], P('dp')
The draws below stay inside these ranges and needn't reach their ends.
Inputs may be any that keep to these rules, and one draw needn't show every extreme that they name: `new_owner`: one index of dp, the departing one, owns no piece. Every index of dp sends 2 or 1 of its pieces to every other surviving index and to itself if it survives, none to the departing one; every surviving index ends with 114 or 113 pieces. `new_slot`: the slots of the pieces of one new owner are distinct.
All inputs are finite; a program needn't handle non-finite values.
Results may differ from the reference program's by a relative error of at most 0.001.
Values may be sent and summed in bfloat16 or wider, within the bound.
No kernel may reach another device: no remote copies, remote signals or barrier semaphores. Data moves between devices by JAX's collectives and lax.ppermute only.
A program may use at most 64 MiB of HBM per device.

```python
import math
import jax
import jax.numpy as jnp

D = 4096
FW = 14336
PIECE = 2
TOKENS = 8192
BLOCKS_DEV = 112
NEWCAP = 114
N_DP = 64


def owner_plan(key):
    remaining_owners = N_DP - 1
    key_leave, key_name_string, key_order = jax.random.split(key, 3)
    leaving = jax.random.randint(key_leave, (), 0, N_DP)
    owner_labels = jax.random.permutation(key_name_string, remaining_owners)
    owner_orderings = jax.vmap(lambda sub: jax.random.permutation(sub, BLOCKS_DEV))(jax.random.split(key_order, N_DP))
    sender_owner = jnp.arange(N_DP, dtype=jnp.int32)[:, None]
    rank_number = sender_owner + N_DP * owner_orderings
    receiver_owner = owner_labels[(sender_owner + owner_orderings) % remaining_owners]
    owner = receiver_owner + (receiver_owner >= leaving).astype(jnp.int32)
    state_slots = rank_number // remaining_owners
    return (owner.reshape(-1).astype(jnp.int32), state_slots.reshape(-1).astype(jnp.int32))


def draw_new_owner(key, part):
    owner, state_slots = owner_plan(key)
    return owner


def draw_new_slot(key, part):
    owner, state_slots = owner_plan(key)
    return state_slots


def steps_of(own_key, extent, shards, low, high):
    level, own = 1.0, jax.random.fold_in(own_key, 6)
    for dim, parts in shards:
        heights = jnp.exp(jax.random.uniform(jax.random.fold_in(own, dim), (parts,), jnp.float32, low / len(shards), high / len(shards)))
        level = level * jnp.repeat(heights, extent[dim] // parts).reshape([-1 if axis == dim else 1 for axis in range(len(extent))])
    return level


def scatter_about(rng, shape, scale, most, cuts=(), kind=jnp.bfloat16):
    array = jax.random.normal(rng, shape, jnp.float32) * scale
    if len(cuts) > 0:
        array = steps_of(rng, shape, cuts, -0.22, 0.18) * array
    return jnp.clip(array, min=-most, max=most).astype(kind)


def setup_inputs(seed: int = 0) -> dict:
    key_list = jax.random.split(jax.random.key(seed), 8)
    activations = scatter_about(key_list[0], (TOKENS, D), 1.0, 6.0, ((0, 64), (1, 8)))
    cotangent = scatter_about(key_list[1], (TOKENS, FW), TOKENS ** -0.5, 0.0625, ((0, 512),))
    master = scatter_about(key_list[2], (FW, D), 1.0, 6.0, ((0, 64), (1, 8)), jnp.float32)
    first_moment = scatter_about(key_list[3], (FW, D), 1.0, 6.0, ((0, 64), (1, 8)), jnp.float32)
    second_moment = jnp.clip(jnp.exp(math.log(4.0) - 2.7725887 * jax.random.uniform(key_list[4], (FW, D), jnp.float32) ** steps_of(key_list[4], (FW, D), ((0, 64), (1, 8)), -0.2, 0.2)), 0.25, 4.0)
    new_owner = draw_new_owner(jax.random.fold_in(key_list[7], 71), 0)
    new_slot = draw_new_slot(jax.random.fold_in(key_list[7], 71), 0)
    return dict(activations=activations, cotangent=cotangent, master=master, first_moment=first_moment, second_moment=second_moment, new_owner=new_owner, new_slot=new_slot)


beta_one = 0.9
beta_two = 0.95
learn_rate = 0.1
adam_eps = 1e-08
adam_step = 1000
fix_one = 1.0 - beta_one ** adam_step
fix_two = 1.0 - beta_two ** adam_step

def relay_rows(field, new_owner, new_slot):
    width = field.shape[1]
    blocks = field.reshape(-1, PIECE * width)
    position = (new_owner * NEWCAP + new_slot).astype(jnp.int32)
    placed = jnp.zeros((N_DP * NEWCAP, PIECE * width), field.dtype).at[position].set(blocks)
    return placed.reshape(N_DP * NEWCAP * PIECE, width)

def reference(activations, cotangent, master, first_moment, second_moment, new_owner, new_slot):
    grad = jnp.dot(cotangent.T, activations, preferred_element_type=jnp.float32)
    moment1_next = beta_one * first_moment + (1.0 - beta_one) * grad
    moment2_next = beta_two * second_moment + (1.0 - beta_two) * grad * grad
    update = learn_rate * (moment1_next / fix_one) / (jnp.sqrt(moment2_next / fix_two) + adam_eps)
    master_next = master - update
    new_master = relay_rows(master_next, new_owner, new_slot)
    new_moment1 = relay_rows(moment1_next, new_owner, new_slot)
    new_moment2 = relay_rows(moment2_next, new_owner, new_slot)
    return (new_master, new_moment1, new_moment2, new_master.astype(jnp.bfloat16))
```

```python
import functools

import jax
import jax.numpy as jnp
import numpy as np
from jax import lax
from jax.experimental import pallas as pl
from jax.experimental.pallas import tpu as pltpu
from jax.sharding import Mesh, PartitionSpec as P

beta_one = 0.9
beta_two = 0.95
learn_rate = 0.1
adam_eps = 1e-08
adam_step = 1000
fix_one = 1.0 - beta_one**adam_step
fix_two = 1.0 - beta_two**adam_step

Z, X, CORES, Y = 8, 4, 2, 8
CHIPS = Z * X
DP = CHIPS * CORES
ROWS = 224
PAD = 256
PIECES = 112
PAIR = 2
CAP = 114
WIDTH = 512

VMEM = pl.BlockSpec(memory_space=pltpu.VMEM)
SMEM = pl.BlockSpec(memory_space=pltpu.SMEM)
LIMIT = 56 * 1024 * 1024


def call(kernel, out_shape, in_specs, out_specs, **kw):
    return pl.pallas_call(
        kernel,
        out_shape=out_shape,
        in_specs=in_specs,
        out_specs=out_specs,
        compiler_params=pltpu.CompilerParams(vmem_limit_bytes=LIMIT),
        **kw,
    )


def pack_cotangent(core_ref, cot_ref, out_ref):
    tokens = cot_ref.shape[0]
    blank = jnp.zeros((tokens, PAD - ROWS), jnp.bfloat16)

    def fill(flip):
        for chip in range(CHIPS):
            for core in range(CORES):
                start = ROWS * (CORES * chip + core)
                block = jnp.concatenate([cot_ref[:, start : start + ROWS], blank], axis=1)
                place = PAD * (core ^ flip)
                out_ref[chip, :, place : place + PAD] = block

    @pl.when(core_ref[0] == 0)
    def _():
        fill(0)

    @pl.when(core_ref[0] == 1)
    def _():
        fill(1)


def pack_pieces(position_ref, field_ref, out_ref):
    out_ref[...] = jnp.zeros_like(out_ref)
    for piece in range(PIECES):
        out_ref[position_ref[piece]] = field_ref[PAIR * piece : PAIR * piece + PAIR, :]


def pack_states(position_ref, a_ref, b_ref, c_ref, out_ref):
    out_ref[...] = jnp.zeros_like(out_ref)
    for piece in range(PIECES):
        place = position_ref[piece]
        for index, ref in enumerate((a_ref, b_ref, c_ref)):
            out_ref[place, :, WIDTH * index : WIDTH * (index + 1)] = ref[PAIR * piece : PAIR * piece + PAIR, :]


def pack_grad(position_ref, mine_ref, theirs_ref, out_ref):
    out_ref[...] = jnp.zeros_like(out_ref)
    for piece in range(PIECES):
        rows = slice(PAIR * piece, PAIR * piece + PAIR)
        out_ref[position_ref[piece]] = mine_ref[rows, :] + theirs_ref[rows, :]


def partial_grad(me_ref, cot_ref, own_ref, left_ref, low_ref, high_ref, right_ref, after_ref, mine_ref, theirs_ref):
    step = pl.program_id(0)
    me = me_ref[0]

    def tokens(offset):
        return cot_ref[0, :, lax.rem(me + offset, X)].reshape(Z * 16, 2 * PAD)

    cot = jnp.concatenate([tokens(0), tokens(X - 1), tokens(2), tokens(1)], axis=0)
    parts = (own_ref, left_ref, low_ref, high_ref, right_ref)
    act = jnp.concatenate([ref[...].reshape(-1, WIDTH) for ref in parts], axis=0)
    part = lax.dot_general(cot, act, (((0,), (0,)), ((), ())), preferred_element_type=jnp.float32)

    @pl.when(step == 0)
    def _():
        mine_ref[...] = part[:ROWS]
        theirs_ref[...] = part[PAD : PAD + ROWS]

    @pl.when(step > 0)
    def _():
        mine_ref[...] += part[:ROWS]
        theirs_ref[...] += part[PAD : PAD + ROWS]


def place_states(slot_ref, arrived_ref, a_ref, b_ref, c_ref, placed):
    placed[...] = jnp.zeros_like(placed)
    for entry in range(DP * PAIR):
        placed[slot_ref[entry]] = arrived_ref[entry]
    for index, ref in enumerate((a_ref, b_ref, c_ref)):
        ref[...] = placed[:CAP, :, WIDTH * index : WIDTH * (index + 1)].reshape(PAIR * CAP, WIDTH)


def finish(slot_ref, grad_ref, master_ref, moment1_ref, moment2_ref, a_ref, b_ref, c_ref, w_ref, placed):
    placed[...] = jnp.zeros_like(placed)
    for entry in range(DP * PAIR):
        placed[slot_ref[entry]] = grad_ref[entry]
    grad = placed[:CAP].reshape(PAIR * CAP, WIDTH)
    moment1 = beta_one * moment1_ref[...] + (1.0 - beta_one) * grad
    moment2 = beta_two * moment2_ref[...] + (1.0 - beta_two) * grad * grad
    update = learn_rate * (moment1 / fix_one) / (jnp.sqrt(moment2 / fix_two) + adam_eps)
    master = master_ref[...] - update
    a_ref[...] = master
    b_ref[...] = moment1
    c_ref[...] = moment2
    w_ref[...] = master.astype(jnp.bfloat16)


def f32(*shape):
    return jax.ShapeDtypeStruct(shape, jnp.float32)


def bf16(*shape):
    return jax.ShapeDtypeStruct(shape, jnp.bfloat16)


def shards(activations, cotangent, master, first_moment, second_moment, new_owner, new_slot):
    core = lax.axis_index("c").astype(jnp.int32).reshape(1)
    act_z = lax.all_gather(activations, "z", axis=0, tiled=True)
    right = [(i, (i + 1) % X) for i in range(X)]
    left = [(i, (i - 1) % X) for i in range(X)]
    half = act_z.shape[0] // 2
    from_left = lax.ppermute(act_z, "x", right)
    from_right = lax.ppermute(act_z, "x", left)
    far_low = lax.ppermute(from_left[:half], "x", right)
    far_high = lax.ppermute(from_right[half:], "x", left)

    packed = call(pack_cotangent, bf16(CHIPS, 16, 2 * PAD), [SMEM, VMEM], VMEM)(core, cotangent)
    shared = lax.all_to_all(packed, ("z", "x"), split_axis=0, concat_axis=0, tiled=True)
    cotangent_all = lax.all_gather(shared.reshape(CHIPS * 16, 2 * PAD), "y", axis=0)

    matching = new_owner[:, None] == new_owner[None, :]
    counter = jnp.arange(PIECES, dtype=jnp.int32)
    earlier = counter[None, :] < counter[:, None]
    rank_number = jnp.sum((matching & earlier).astype(jnp.int32), axis=1)
    position = new_owner * PAIR + rank_number
    hits = position[None, :] == jnp.arange(DP * PAIR, dtype=jnp.int32)[:, None]
    slots = jnp.sum(jnp.where(hits, new_slot[None, :] - CAP, 0), axis=1) + CAP
    dp_axes = ("z", "x", "c")
    slots = lax.all_to_all(slots.reshape(DP, 1, PAIR), dp_axes, split_axis=0, concat_axis=0, tiled=True)
    slots = slots.reshape(DP * PAIR)

    states = call(pack_states, f32(DP * PAIR, PAIR, 3 * WIDTH), [SMEM, VMEM, VMEM, VMEM], VMEM)(
        position, master, first_moment, second_moment
    )
    arrived = lax.all_to_all(states, dp_axes, split_axis=0, concat_axis=0, tiled=True)
    placed = call(place_states, (f32(PAIR * CAP, WIDTH),) * 3, [SMEM, VMEM], (VMEM,) * 3, scratch_shapes=[pltpu.VMEM((CAP + 1, PAIR, 3 * WIDTH), jnp.float32)])(
        slots, arrived
    )

    me = lax.axis_index("x").astype(jnp.int32).reshape(1)
    full = pl.BlockSpec((Z, 1, 16, WIDTH), lambda i: (0, i, 0, 0))
    some = pl.BlockSpec((Z // 2, 1, 16, WIDTH), lambda i: (0, i, 0, 0))
    mine, theirs = pl.pallas_call(
        partial_grad,
        grid=(Y,),
        out_shape=(f32(ROWS, WIDTH),) * 2,
        in_specs=[
            SMEM,
            pl.BlockSpec((1, Z, X, 16, 2 * PAD), lambda i: (i, 0, 0, 0, 0)),
            full,
            full,
            some,
            some,
            full,
            pl.BlockSpec(memory_space=pl.ANY),
        ],
        out_specs=[pl.BlockSpec((ROWS, WIDTH), lambda i: (0, 0))] * 2,
        compiler_params=pltpu.CompilerParams(vmem_limit_bytes=LIMIT),
    )(
        me,
        cotangent_all.reshape(Y, Z, X, 16, 2 * PAD),
        *[part.reshape(-1, Y, 16, WIDTH) for part in (act_z, from_left, far_low, far_high, from_right)],
        placed[0],
    )
    theirs = lax.ppermute(theirs, "c", [(0, 1), (1, 0)])
    grads = call(pack_grad, f32(DP * PAIR, PAIR, WIDTH), [SMEM, VMEM, VMEM], VMEM)(position, mine, theirs)
    grads = lax.all_to_all(grads, dp_axes, split_axis=0, concat_axis=0, tiled=True)
    new_master, new_moment1, new_moment2, weights = call(
        finish,
        (f32(PAIR * CAP, WIDTH),) * 3 + (bf16(PAIR * CAP, WIDTH),),
        [SMEM] + [VMEM] * 4,
        (VMEM,) * 4,
        scratch_shapes=[pltpu.VMEM((CAP + 1, PAIR, WIDTH), jnp.float32)],
    )(slots, grads, *placed)
    new_weights = lax.all_gather(weights, "y", axis=1, tiled=True)
    return (new_master, new_moment1, new_moment2, new_weights)


def solution(mesh):
    fine = Mesh(np.asarray(mesh.devices).reshape(Z, X, CORES, Y), ("z", "x", "c", "y"))
    dp = ("z", "x", "c")
    in_specs = (
        P(dp, "y"),
        P(dp + ("y",), None),
        P(dp, "y"),
        P(dp, "y"),
        P(dp, "y"),
        P(dp),
        P(dp),
    )
    out_specs = (P(dp, "y"), P(dp, "y"), P(dp, "y"), P(dp, None))
    return jax.shard_map(shards, mesh=fine, in_specs=in_specs, out_specs=out_specs, check_vma=False)
```

```python
import jax
import jax.numpy as jnp
import numpy as np
from jax import lax
from jax.experimental import pallas as pl
from jax.experimental.pallas import tpu as pltpu
from jax.sharding import Mesh, PartitionSpec as P

beta_one = 0.9
beta_two = 0.95
learn_rate = 0.1
adam_eps = 1e-08
adam_step = 1000
fix_one = 1.0 - beta_one**adam_step
fix_two = 1.0 - beta_two**adam_step

Z, X, CORES, Y = 8, 4, 2, 8
CHIPS = Z * X
DP = CHIPS * CORES
ROWS = 224
PAD = 256
PIECES = 112
PAIR = 2
CAP = 114
WIDTH = 512
LANES = 128
SCALES = (1024.0, 64.0, 0.0625)

VMEM = pl.BlockSpec(memory_space=pltpu.VMEM)
SMEM = pl.BlockSpec(memory_space=pltpu.SMEM)
ANY = pl.BlockSpec(memory_space=pl.ANY)
LIMIT = 16 * 1024 * 1024


def call(kernel, out_shape, in_specs, out_specs, flops=0, **kw):
    return pl.pallas_call(
        kernel,
        out_shape=out_shape,
        in_specs=in_specs,
        out_specs=out_specs,
        cost_estimate=pl.CostEstimate(flops=flops, bytes_accessed=4 << 20, transcendentals=0),
        compiler_params=pltpu.CompilerParams(vmem_limit_bytes=LIMIT),
        **kw,
    )


def pack_cotangent(core_ref, cot_ref, out_ref):
    blank = jnp.zeros((cot_ref.shape[0], PAD - ROWS), jnp.bfloat16)

    def fill(flip):
        for device in range(DP):
            start = ROWS * device
            block = jnp.concatenate([cot_ref[:, start : start + ROWS], blank], axis=1)
            place = PAD * ((device % CORES) ^ flip)
            out_ref[device // CORES, :, place : place + PAD] = block

    @pl.when(core_ref[0] == 0)
    def _():
        fill(0)

    @pl.when(core_ref[0] == 1)
    def _():
        fill(1)


def plan(owner_ref, slot_ref, position_ref, entry_slot_ref):
    shape = (LANES, LANES)

    def padded(ref):
        return jnp.concatenate([ref[...], jnp.full((1, LANES - PIECES), -1, jnp.int32)], axis=1)

    def column(row):
        return jnp.broadcast_to(row.astype(jnp.float32), shape).T.astype(jnp.int32)

    owner = padded(owner_ref)
    first, second = (lax.broadcasted_iota(jnp.int32, shape, dim) for dim in (0, 1))
    same = jnp.where((column(owner) == owner) & (first < second), 1, 0)
    rank = jnp.sum(same, axis=0, keepdims=True)
    lane = lax.broadcasted_iota(jnp.int32, (1, LANES), 1)
    position = jnp.where(lane < PIECES, owner * PAIR + rank, -1)
    position_ref[...] = position
    found = jnp.where(column(position) == second, column(padded(slot_ref)) - CAP, 0)
    entry_slot_ref[...] = jnp.sum(found, axis=0, keepdims=True) + CAP


def add_blocks(total, scratch, me_ref, parts, blocks):
    cot_buf, act_buf, cot_sem, act_sem = scratch
    me, x = me_ref[0], me_ref[1]
    half = Z // 2
    places = [(0, Z, 0), (0, Z, X - 1), (0, Z, 1), (0, half, 2), (half, half, 2)]
    plans, number = [], 0
    for block, (step, refs) in enumerate(blocks):
        index = lax.rem(me + (Y + step), Y)
        copies, start = [], 0
        for part, (low, count, offset) in enumerate(places):
            target = act_buf.at[block, pl.ds(low, count), lax.rem(x + offset, X)]
            copies.append(pltpu.make_async_copy(parts[part].at[:, index], target, act_sem.at[block, part]))
        for ref in refs:
            target = cot_buf.at[block, pl.ds(start, ref.shape[0])]
            copies.append(pltpu.make_async_copy(ref, target, cot_sem.at[number]))
            start, number = start + ref.shape[0], number + 1
        plans.append(copies)
    for copies in plans:
        for copy in copies:
            copy.start()
    for block, copies in enumerate(plans):
        for copy in copies:
            copy.wait()
        act = act_buf[block].reshape(CHIPS * 16, WIDTH)
        part = lax.dot_general(
            cot_buf[block], act, (((0,), (0,)), ((), ())), preferred_element_type=jnp.float32
        )
        total = part if total is None else total + part
    return total


def first_blocks(me_ref, a0, a1, a2, a3, a4, own, down1, up1, down2, up2, after_ref, out_ref, *scratch):
    blocks = [(0, [own]), (-1, [down1]), (1, [up1]), (-2, [down2]), (2, [up2])]
    out_ref[...] = add_blocks(None, scratch, me_ref, (a0, a1, a2, a3, a4), blocks)


def last_blocks(me_ref, a0, a1, a2, a3, a4, before_ref, down3, up3, upper, lower, mine_ref, theirs_ref, *scratch):
    blocks = [(-3, [down3]), (3, [up3]), (4, [upper, lower])]
    total = add_blocks(before_ref[...], scratch, me_ref, (a0, a1, a2, a3, a4), blocks)
    mine_ref[...] = total[:ROWS]
    theirs_ref[...] = total[PAD : PAD + ROWS]


def block_scratch(blocks, copies):
    return [
        pltpu.VMEM((blocks, CHIPS * 16, 2 * PAD), jnp.bfloat16),
        pltpu.VMEM((blocks, Z, X, 16, WIDTH), jnp.bfloat16),
        pltpu.SemaphoreType.DMA((copies,)),
        pltpu.SemaphoreType.DMA((blocks, 5)),
    ]


def update_state(mine_ref, theirs_ref, master_ref, moment1_ref, moment2_ref):
    grad = mine_ref[...] + theirs_ref[...]
    moment1 = beta_one * moment1_ref[...] + (1.0 - beta_one) * grad
    moment2 = beta_two * moment2_ref[...] + (1.0 - beta_two) * grad * grad
    update = learn_rate * (moment1 / fix_one) / (jnp.sqrt(moment2 / fix_two) + adam_eps)
    return master_ref[...] - update, moment1, moment2


def step_weights(position_ref, mine_ref, theirs_ref, master_ref, moment1_ref, moment2_ref, out_ref, master):
    master[...] = update_state(mine_ref, theirs_ref, master_ref, moment1_ref, moment2_ref)[0]
    out_ref[...] = jnp.zeros_like(out_ref)
    for piece in range(PIECES):
        rows = master[PAIR * piece : PAIR * piece + PAIR, :]
        out_ref[position_ref[0, piece]] = rows.astype(jnp.bfloat16)


def step_states(position_ref, mine_ref, theirs_ref, master_ref, moment1_ref, moment2_ref, out_ref, state):
    fields = update_state(mine_ref, theirs_ref, master_ref, moment1_ref, moment2_ref)
    for index, field in enumerate(fields):
        state[index] = field * SCALES[index]
    out_ref[...] = jnp.zeros_like(out_ref)
    for piece in range(PIECES):
        place = position_ref[0, piece]
        for index in range(3):
            rows = state[index, PAIR * piece : PAIR * piece + PAIR, :]
            out_ref[place, :, WIDTH * index : WIDTH * (index + 1)] = rows


def place_states(slot_ref, arrived_ref, a_ref, b_ref, c_ref, placed):
    placed[...] = jnp.zeros_like(placed)
    for entry in range(DP * PAIR):
        placed[slot_ref[entry]] = arrived_ref[entry]
    for index, ref in enumerate((a_ref, b_ref, c_ref)):
        rows = placed[:CAP, :, WIDTH * index : WIDTH * (index + 1)].reshape(PAIR * CAP, WIDTH)
        ref[...] = rows * (1.0 / SCALES[index])


def place_weights(slot_ref, arrived_ref, out_ref, placed):
    placed[...] = jnp.zeros_like(placed)
    for entry in range(DP * PAIR):
        placed[slot_ref[entry]] = arrived_ref[entry].astype(jnp.float32)
    out_ref[...] = placed[:CAP].reshape(PAIR * CAP, WIDTH).astype(jnp.bfloat16)


def hold(value_ref, after_ref, out_ref):
    del value_ref, after_ref, out_ref


def f32(*shape):
    return jax.ShapeDtypeStruct(shape, jnp.float32)


def int32(*shape):
    return jax.ShapeDtypeStruct(shape, jnp.int32)


def bf16(*shape):
    return jax.ShapeDtypeStruct(shape, jnp.bfloat16)


def shards(activations, cotangent, master, first_moment, second_moment, new_owner, new_slot):
    dp_axes = ("z", "x", "c")
    core = lax.axis_index("c").astype(jnp.int32).reshape(1)
    packed = call(pack_cotangent, bf16(CHIPS, 16, 2 * PAD), [SMEM, VMEM], VMEM)(core, cotangent)
    shared = lax.all_to_all(packed, ("z", "x"), split_axis=0, concat_axis=0, tiled=True)
    shared = shared.reshape(CHIPS * 16, 2 * PAD)

    act = lax.all_gather(activations, "z", axis=0, tiled=True)
    right = [(i, (i + 1) % X) for i in range(X)]
    left = [(i, (i - 1) % X) for i in range(X)]
    half = act.shape[0] // 2
    acts = [act, lax.ppermute(act, "x", right), lax.ppermute(act, "x", left)]
    acts += [lax.ppermute(acts[1][:half], "x", right), lax.ppermute(acts[2][half:], "x", left)]
    acts = [part.reshape(-1, Y, 16, WIDTH) for part in acts]

    right = [(i, (i + 1) % Y) for i in range(Y)]
    left = [(i, (i - 1) % Y) for i in range(Y)]
    down, up = [shared], [shared]
    for _ in range(Y // 2 - 1):
        down.append(lax.ppermute(down[-1], "y", right))
        up.append(lax.ppermute(up[-1], "y", left))
    far = [lax.ppermute(down[-1][:PAD], "y", right), lax.ppermute(up[-1][PAD:], "y", left)]

    position, slots = call(plan, (int32(1, LANES),) * 2, [VMEM] * 2, (VMEM,) * 2)(
        new_owner.reshape(1, PIECES), new_slot.reshape(1, PIECES)
    )
    slots = lax.all_to_all(slots.reshape(DP, 1, PAIR), dp_axes, split_axis=0, concat_axis=0, tiled=True)
    slots = slots.reshape(DP * PAIR)

    me = jnp.stack([lax.axis_index("y"), lax.axis_index("x")]).astype(jnp.int32)
    partial = call(
        first_blocks,
        f32(2 * PAD, WIDTH),
        [SMEM] + [ANY] * 11,
        VMEM,
        flops=5 << 29,
        scratch_shapes=block_scratch(5, 5),
    )(me, *acts, shared, down[1], up[1], down[2], up[2], slots)
    mine, theirs = call(
        last_blocks,
        (f32(ROWS, WIDTH),) * 2,
        [SMEM] + [ANY] * 5 + [VMEM] + [ANY] * 4,
        (VMEM,) * 2,
        flops=3 << 29,
        scratch_shapes=block_scratch(3, 4),
    )(me, *acts, partial, down[3], up[3], *far)
    theirs = lax.ppermute(theirs, "c", [(0, 1), (1, 0)])
    step = (position, mine, theirs, master, first_moment, second_moment)
    weights = call(
        step_weights,
        bf16(DP * PAIR, PAIR, WIDTH),
        [SMEM] + [VMEM] * 5,
        VMEM,
        scratch_shapes=[pltpu.VMEM((ROWS, WIDTH), jnp.float32)],
    )(*step)

    weights = lax.all_to_all(weights, dp_axes, split_axis=0, concat_axis=0, tiled=True)
    weights = call(
        place_weights,
        bf16(PAIR * CAP, WIDTH),
        [SMEM, VMEM],
        VMEM,
        scratch_shapes=[pltpu.VMEM((CAP + 1, PAIR, WIDTH), jnp.float32)],
    )(slots, weights)
    new_weights = lax.all_gather(weights, "y", axis=1, tiled=True)

    states = call(
        step_states,
        f32(DP * PAIR, PAIR, 3 * WIDTH),
        [SMEM] + [VMEM] * 5,
        VMEM,
        flops=1 << 31,
        scratch_shapes=[pltpu.VMEM((3, ROWS, WIDTH), jnp.float32)],
    )(*step)
    states = call(hold, f32(*states.shape), [ANY, ANY], ANY, input_output_aliases={0: 0})(states, weights)
    states = states.astype(jnp.float16)
    arrived = lax.all_to_all(states, dp_axes, split_axis=0, concat_axis=0, tiled=True)
    placed = call(
        place_states,
        (f32(PAIR * CAP, WIDTH),) * 3,
        [SMEM, VMEM],
        (VMEM,) * 3,
        scratch_shapes=[pltpu.VMEM((CAP + 1, PAIR, 3 * WIDTH), jnp.float32)],
    )(slots, arrived.astype(jnp.float32))
    return (*placed, new_weights)


def solution(mesh):
    fine = Mesh(np.asarray(mesh.devices).reshape(Z, X, CORES, Y), ("z", "x", "c", "y"))
    dp = ("z", "x", "c")
    in_specs = (
        P(dp, "y"),
        P(dp + ("y",), None),
        P(dp, "y"),
        P(dp, "y"),
        P(dp, "y"),
        P(dp),
        P(dp),
    )
    out_specs = (P(dp, "y"), P(dp, "y"), P(dp, "y"), P(dp, None))
    return jax.shard_map(shards, mesh=fine, in_specs=in_specs, out_specs=out_specs, check_vma=False)
```

```python
import jax
import jax.numpy as jnp
import numpy as np
from jax import lax
from jax.experimental import pallas as pl
from jax.experimental.pallas import tpu as pltpu
from jax.sharding import Mesh, PartitionSpec as P

beta_one = 0.9
beta_two = 0.95
learn_rate = 0.1
adam_eps = 1e-08
adam_step = 1000
fix_one = 1.0 - beta_one**adam_step
fix_two = 1.0 - beta_two**adam_step

Z, X, CORES, Y = 8, 4, 2, 8
CHIPS = Z * X
DP = CHIPS * CORES
ROWS = 224
PAD = 256
PIECES = 112
PAIR = 2
CAP = 114
WIDTH = 512
LANES = 128
AHEAD = 3
SCALES = (1024.0, 64.0, 0.0625)

VMEM = pl.BlockSpec(memory_space=pltpu.VMEM)
SMEM = pl.BlockSpec(memory_space=pltpu.SMEM)
ANY = pl.BlockSpec(memory_space=pl.ANY)
LIMIT = 16 * 1024 * 1024
WIDE_LIMIT = 60 * 1024 * 1024


def call(kernel, out_shape, in_specs, out_specs, flops=0, limit=LIMIT, **kw):
    return pl.pallas_call(
        kernel,
        out_shape=out_shape,
        in_specs=in_specs,
        out_specs=out_specs,
        cost_estimate=pl.CostEstimate(flops=flops, bytes_accessed=4 << 20, transcendentals=0),
        compiler_params=pltpu.CompilerParams(vmem_limit_bytes=limit),
        **kw,
    )


def plan(owner_ref, slot_ref):
    shape = (LANES, LANES)

    def padded(ref):
        return jnp.concatenate([ref[...], jnp.full((1, LANES - PIECES), -1, jnp.int32)], axis=1)

    def column(row):
        return jnp.broadcast_to(row.astype(jnp.float32), shape).T.astype(jnp.int32)

    owner = padded(owner_ref)
    first, second = (lax.broadcasted_iota(jnp.int32, shape, dim) for dim in (0, 1))
    same = jnp.where((column(owner) == owner) & (first < second), 1, 0)
    rank = jnp.sum(same, axis=0, keepdims=True)
    lane = lax.broadcasted_iota(jnp.int32, (1, LANES), 1)
    position = jnp.where(lane < PIECES, owner * PAIR + rank, -1)
    found = jnp.where(column(position) == second, column(padded(slot_ref)) - CAP, 0)
    return position, jnp.sum(found, axis=0, keepdims=True) + CAP


def pack_cotangent(core_ref, owner_ref, slot_ref, cot_ref, out_ref, position_ref):
    position, slots = plan(owner_ref, slot_ref)
    position_ref[...] = position
    tokens = cot_ref.shape[0]
    slots = jnp.broadcast_to(slots.astype(jnp.float32), (tokens, LANES))
    spare = PAD - ROWS
    tail = lax.broadcasted_iota(jnp.int32, (tokens, LANES), 1) >= LANES - spare

    def fill(flip):
        for device in range(DP):
            start = ROWS * device
            entries = pltpu.roll(slots, (LANES - spare - PAIR * device) % LANES, 1)
            last = jnp.concatenate([cot_ref[:, start + LANES : start + ROWS], jnp.zeros((tokens, spare), jnp.bfloat16)], axis=1)
            last = jnp.where(tail, entries, last.astype(jnp.float32)).astype(jnp.bfloat16)
            place = PAD * ((device % CORES) ^ flip)
            out_ref[device // CORES, :, place : place + LANES] = cot_ref[:, start : start + LANES]
            out_ref[device // CORES, :, place + LANES : place + PAD] = last

    @pl.when(core_ref[0] == 0)
    def _():
        fill(0)

    @pl.when(core_ref[0] == 1)
    def _():
        fill(1)


def partial_grad(me_ref, act_ref, *refs):
    *parts, mine_ref, theirs_ref, slots_ref, cot_buf, act_buf, cot_sem, act_sem = refs
    steps = [0, -1, 1, -2, 2, -3, 3, 4]
    plans = []
    for block, step in enumerate(steps):
        index = lax.rem(me_ref[0] + (Y + step), Y)
        plans.append([pltpu.make_async_copy(act_ref.at[:, index], act_buf.at[block], act_sem.at[block])])
    for number, ref in enumerate(parts):
        block, start = min(number, Y - 1), PAD if number == Y else 0
        target = cot_buf.at[block, pl.ds(start, ref.shape[0])]
        plans[block].append(pltpu.make_async_copy(ref, target, cot_sem.at[number]))
    for copies in plans[:AHEAD]:
        for copy in copies:
            copy.start()
    total = None
    for block, copies in enumerate(plans):
        for copy in copies:
            copy.wait()
        for copy in plans[block + AHEAD] if block + AHEAD < Y else ():
            copy.start()
        act = act_buf[block].reshape(CHIPS * 16, WIDTH)
        part = lax.dot_general(
            cot_buf[block], act, (((0,), (0,)), ((), ())), preferred_element_type=jnp.float32
        )
        total = part if total is None else total + part
    mine_ref[...] = total[:ROWS]
    theirs_ref[:ROWS] = total[PAD : PAD + ROWS]

    def received(start):
        tile = cot_buf[0, :, start + LANES : start + PAD].astype(jnp.float32).reshape(CHIPS, 16, LANES)[:, 0]
        square = jnp.concatenate([tile, jnp.zeros((LANES - CHIPS, LANES), jnp.float32)], axis=0)
        return square.T[LANES - (PAD - ROWS) :][:8]

    slots_ref[...] = received(0)
    theirs_ref[ROWS:, :LANES] = received(PAD)
    theirs_ref[ROWS:, LANES:] = jnp.zeros((8, WIDTH - LANES), jnp.float32)


def update_state(mine_ref, theirs_ref, master_ref, moment1_ref, moment2_ref):
    grad = mine_ref[...] + theirs_ref[:ROWS]
    moment1 = beta_one * moment1_ref[...] + (1.0 - beta_one) * grad
    moment2 = beta_two * moment2_ref[...] + (1.0 - beta_two) * grad * grad
    update = learn_rate * (moment1 / fix_one) / (jnp.sqrt(moment2 / fix_two) + adam_eps)
    return master_ref[...] - update, moment1, moment2


def step_weights(
    position_ref, mine_ref, theirs_ref, master_ref, moment1_ref, moment2_ref, core_ref, slots_ref, out_ref, table_ref, master
):
    for core in range(CORES):
        rows = jnp.where(core_ref[0] == core, slots_ref[:PAIR], theirs_ref[ROWS : ROWS + PAIR, :LANES])
        table_ref[PAIR * core : PAIR * core + PAIR] = rows.astype(jnp.int32)
    master[...] = update_state(mine_ref, theirs_ref, master_ref, moment1_ref, moment2_ref)[0]
    out_ref[...] = jnp.zeros_like(out_ref)
    for piece in range(PIECES):
        rows = master[PAIR * piece : PAIR * piece + PAIR, :]
        out_ref[position_ref[0, piece]] = rows.astype(jnp.bfloat16)


def step_states(position_ref, mine_ref, theirs_ref, master_ref, moment1_ref, moment2_ref, out_ref, state):
    fields = update_state(mine_ref, theirs_ref, master_ref, moment1_ref, moment2_ref)
    for index, field in enumerate(fields):
        state[index] = field * SCALES[index]
    out_ref[...] = jnp.zeros_like(out_ref)
    for piece in range(PIECES):
        place = position_ref[0, piece]
        for index in range(3):
            rows = state[index, PAIR * piece : PAIR * piece + PAIR, :]
            out_ref[place, :, WIDTH * index : WIDTH * (index + 1)] = rows


def place_states(slot_ref, arrived_ref, a_ref, b_ref, c_ref, placed):
    placed[...] = jnp.zeros_like(placed)
    for entry in range(DP * PAIR):
        placed[slot_ref[entry % 4, entry // 4]] = arrived_ref[entry]
    for index, ref in enumerate((a_ref, b_ref, c_ref)):
        rows = placed[:CAP, :, WIDTH * index : WIDTH * (index + 1)].reshape(PAIR * CAP, WIDTH)
        ref[...] = rows * (1.0 / SCALES[index])


def place_weights(slot_ref, arrived_ref, out_ref, placed):
    placed[...] = jnp.zeros_like(placed)
    for entry in range(DP * PAIR):
        placed[slot_ref[entry % 4, entry // 4]] = arrived_ref[entry].astype(jnp.float32)
    out_ref[...] = placed[:CAP].reshape(PAIR * CAP, WIDTH).astype(jnp.bfloat16)


def hold(value_ref, after_ref, out_ref):
    del value_ref, after_ref, out_ref


def f32(*shape):
    return jax.ShapeDtypeStruct(shape, jnp.float32)


def int32(*shape):
    return jax.ShapeDtypeStruct(shape, jnp.int32)


def bf16(*shape):
    return jax.ShapeDtypeStruct(shape, jnp.bfloat16)


def shards(activations, cotangent, master, first_moment, second_moment, new_owner, new_slot):
    dp_axes = ("z", "x", "c")
    core = lax.axis_index("c").astype(jnp.int32).reshape(1)
    packed, position = call(
        pack_cotangent, (bf16(CHIPS, 16, 2 * PAD), int32(1, LANES)), [SMEM] + [VMEM] * 3, (VMEM,) * 2
    )(core, new_owner.reshape(1, PIECES), new_slot.reshape(1, PIECES), cotangent)
    shared = lax.all_to_all(packed, ("z", "x"), split_axis=0, concat_axis=0, tiled=True)
    shared = shared.reshape(CHIPS * 16, 2 * PAD)

    act = lax.all_gather(activations, ("z", "x"), axis=0, tiled=True).reshape(CHIPS, Y, 16, WIDTH)

    right = [(i, (i + 1) % Y) for i in range(Y)]
    left = [(i, (i - 1) % Y) for i in range(Y)]
    down, up = [shared], [shared]
    for _ in range(Y // 2 - 1):
        down.append(lax.ppermute(down[-1], "y", right))
        up.append(lax.ppermute(up[-1], "y", left))
    far = [lax.ppermute(down[-1][:PAD], "y", right), lax.ppermute(up[-1][PAD:], "y", left)]

    me = lax.axis_index("y").astype(jnp.int32).reshape(1)
    mine, theirs, slots = call(
        partial_grad,
        (f32(ROWS, WIDTH), f32(ROWS + 8, WIDTH), f32(8, LANES)),
        [SMEM] + [ANY] * 10,
        (VMEM,) * 3,
        flops=1 << 32,
        limit=WIDE_LIMIT,
        scratch_shapes=[
            pltpu.VMEM((Y, CHIPS * 16, 2 * PAD), jnp.bfloat16),
            pltpu.VMEM((Y, CHIPS, 16, WIDTH), jnp.bfloat16),
            pltpu.SemaphoreType.DMA((Y + 1,)),
            pltpu.SemaphoreType.DMA((Y,)),
        ],
    )(me, act, shared, down[1], up[1], down[2], up[2], down[3], up[3], *far)
    theirs = lax.ppermute(theirs, "c", [(0, 1), (1, 0)])
    step = (position, mine, theirs, master, first_moment, second_moment)
    weights, slots = call(
        step_weights,
        (bf16(DP * PAIR, PAIR, WIDTH), int32(CORES * PAIR, LANES)),
        [SMEM] + [VMEM] * 5 + [SMEM, VMEM],
        (VMEM,) * 2,
        scratch_shapes=[pltpu.VMEM((ROWS, WIDTH), jnp.float32)],
    )(*step, core, slots)

    weights = lax.all_to_all(weights, dp_axes, split_axis=0, concat_axis=0, tiled=True)
    weights = call(
        place_weights,
        bf16(PAIR * CAP, WIDTH),
        [SMEM, VMEM],
        VMEM,
        scratch_shapes=[pltpu.VMEM((CAP + 1, PAIR, WIDTH), jnp.float32)],
    )(slots, weights)
    new_weights = lax.all_gather(weights, "y", axis=1, tiled=True)

    states = call(
        step_states,
        f32(DP * PAIR, PAIR, 3 * WIDTH),
        [SMEM] + [VMEM] * 5,
        VMEM,
        flops=1 << 31,
        scratch_shapes=[pltpu.VMEM((3, ROWS, WIDTH), jnp.float32)],
    )(*step)
    states = call(hold, f32(*states.shape), [ANY, ANY], ANY, input_output_aliases={0: 0})(states, weights)
    states = states.astype(jnp.float16)
    arrived = lax.all_to_all(states, dp_axes, split_axis=0, concat_axis=0, tiled=True)
    placed = call(
        place_states,
        (f32(PAIR * CAP, WIDTH),) * 3,
        [SMEM, VMEM],
        (VMEM,) * 3,
        scratch_shapes=[pltpu.VMEM((CAP + 1, PAIR, 3 * WIDTH), jnp.float32)],
    )(slots, arrived.astype(jnp.float32))
    return (*placed, new_weights)


def solution(mesh):
    fine = Mesh(np.asarray(mesh.devices).reshape(Z, X, CORES, Y), ("z", "x", "c", "y"))
    dp = ("z", "x", "c")
    in_specs = (
        P(dp, "y"),
        P(dp + ("y",), None),
        P(dp, "y"),
        P(dp, "y"),
        P(dp, "y"),
        P(dp),
        P(dp),
    )
    out_specs = (P(dp, "y"), P(dp, "y"), P(dp, "y"), P(dp, None))
    return jax.shard_map(shards, mesh=fine, in_specs=in_specs, out_specs=out_specs, check_vma=False)
```

```python
import jax
import jax.numpy as jnp
import numpy as np
from jax import lax
from jax.experimental import pallas as pl
from jax.experimental.pallas import tpu as pltpu
from jax.sharding import Mesh, PartitionSpec as P

beta_one = 0.9
beta_two = 0.95
learn_rate = 0.1
adam_eps = 1e-08
adam_step = 1000
fix_one = 1.0 - beta_one**adam_step
fix_two = 1.0 - beta_two**adam_step

Z, X, CORES, Y = 8, 4, 2, 8
CHIPS = Z * X
DP = CHIPS * CORES
ROWS = 224
PAD = 256
PIECES = 112
PAIR = 2
CAP = 114
WIDTH = 512
LANES = 128
STEPS = (0, -1, 1, -2, 2, -3, 3, 4)
SCALES = (1024.0, 64.0, 0.0625)

VMEM = pl.BlockSpec(memory_space=pltpu.VMEM)
SMEM = pl.BlockSpec(memory_space=pltpu.SMEM)
ANY = pl.BlockSpec(memory_space=pl.ANY)
LIMIT = 16 * 1024 * 1024
WIDE_LIMIT = 60 * 1024 * 1024


def call(kernel, out_shape, in_specs, out_specs, flops=0, limit=LIMIT, **kw):
    return pl.pallas_call(
        kernel,
        out_shape=out_shape,
        in_specs=in_specs,
        out_specs=out_specs,
        cost_estimate=pl.CostEstimate(flops=flops, bytes_accessed=4 << 20, transcendentals=0),
        compiler_params=pltpu.CompilerParams(vmem_limit_bytes=limit),
        **kw,
    )


def plan(owner_ref, slot_ref):
    shape = (LANES, LANES)

    def padded(ref):
        return jnp.concatenate([ref[...], jnp.full((1, LANES - PIECES), -1, jnp.int32)], axis=1)

    def column(row):
        return jnp.broadcast_to(row.astype(jnp.float32), shape).T.astype(jnp.int32)

    owner = padded(owner_ref)
    first, second = (lax.broadcasted_iota(jnp.int32, shape, dim) for dim in (0, 1))
    same = jnp.where((column(owner) == owner) & (first < second), 1, 0)
    rank = jnp.sum(same, axis=0, keepdims=True)
    lane = lax.broadcasted_iota(jnp.int32, (1, LANES), 1)
    position = jnp.where(lane < PIECES, owner * PAIR + rank, -1)
    found = jnp.where(column(position) == second, column(padded(slot_ref)) - CAP, 0)
    return position, jnp.sum(found, axis=0, keepdims=True) + CAP


def pack_cotangent(core_ref, owner_ref, slot_ref, cot_ref, out_ref, position_ref):
    position, slots = plan(owner_ref, slot_ref)
    position_ref[...] = position
    tokens = cot_ref.shape[0]
    slots = jnp.broadcast_to(slots.astype(jnp.float32), (tokens, LANES))
    spare = PAD - ROWS
    tail = lax.broadcasted_iota(jnp.int32, (tokens, LANES), 1) >= LANES - spare

    def fill(flip):
        for device in range(DP):
            start = ROWS * device
            entries = pltpu.roll(slots, (LANES - spare - PAIR * device) % LANES, 1)
            last = jnp.concatenate([cot_ref[:, start + LANES : start + ROWS], jnp.zeros((tokens, spare), jnp.bfloat16)], axis=1)
            last = jnp.where(tail, entries, last.astype(jnp.float32)).astype(jnp.bfloat16)
            place = PAD * ((device % CORES) ^ flip)
            out_ref[device // CORES, :, place : place + LANES] = cot_ref[:, start : start + LANES]
            out_ref[device // CORES, :, place + LANES : place + PAD] = last

    @pl.when(core_ref[0] == 0)
    def _():
        fill(0)

    @pl.when(core_ref[0] == 1)
    def _():
        fill(1)


def turn(me_ref, *refs):
    *parts, own_ref, other_ref, mine_ref, theirs_ref, tokens = refs
    half = CHIPS // 2
    for number, ref in enumerate(parts):
        index = lax.rem(me_ref[0] + (Y + STEPS[(number + 1) // 2]), Y)
        count = ref.shape[0] // 16
        first = half * ((number + 1) % 2) if number else 0
        tokens[first : first + count, index] = ref[...].reshape(count, 16, 2 * PAD)
    own_ref[...] = tokens[:, :, :, :PAD].reshape(CHIPS * Y * 16, PAD).T[:ROWS]
    other_ref[...] = tokens[:, :, :, PAD:].reshape(CHIPS * Y * 16, PAD).T[:ROWS]

    def received(start):
        tile = parts[0][:, start + LANES : start + PAD].astype(jnp.float32).reshape(CHIPS, 16, LANES)[:, 0]
        square = jnp.concatenate([tile, jnp.zeros((LANES - CHIPS, LANES), jnp.float32)], axis=0)
        return square.T[LANES - (PAD - ROWS) :][:8]

    mine_ref[...] = received(0)
    theirs_ref[...] = received(PAD)


def mine_grad(cot_ref, act_ref, out_ref):
    out_ref[...] = jnp.dot(cot_ref[...], act_ref[...], preferred_element_type=jnp.float32)


def theirs_grad(cot_ref, act_ref, slots_ref, out_ref):
    out_ref[:ROWS] = jnp.dot(cot_ref[...], act_ref[...], preferred_element_type=jnp.float32)
    out_ref[ROWS:, :LANES] = slots_ref[...]
    out_ref[ROWS:, LANES:] = jnp.zeros((8, WIDTH - LANES), jnp.float32)


def copy_columns(in_ref, out_ref, held, in_sem, out_sem):
    copies = []
    for part in range(Y):
        columns = pl.ds(WIDTH * part, WIDTH)
        copies.append(
            (
                pltpu.make_async_copy(in_ref.at[:, columns], held.at[part], in_sem.at[part]),
                pltpu.make_async_copy(held.at[part], out_ref.at[:, columns], out_sem.at[part]),
            )
        )
    for arrive, _ in copies:
        arrive.start()
    for arrive, leave in copies:
        arrive.wait()
        leave.start()
    for _, leave in copies:
        leave.wait()


def update_state(mine_ref, theirs_ref, master_ref, moment1_ref, moment2_ref):
    grad = mine_ref[...] + theirs_ref[:ROWS]
    moment1 = beta_one * moment1_ref[...] + (1.0 - beta_one) * grad
    moment2 = beta_two * moment2_ref[...] + (1.0 - beta_two) * grad * grad
    update = learn_rate * (moment1 / fix_one) / (jnp.sqrt(moment2 / fix_two) + adam_eps)
    return master_ref[...] - update, moment1, moment2


def step_weights(
    position_ref, mine_ref, theirs_ref, master_ref, moment1_ref, moment2_ref, core_ref, slots_ref, out_ref, table_ref, master
):
    for core in range(CORES):
        rows = jnp.where(core_ref[0] == core, slots_ref[:PAIR], theirs_ref[ROWS : ROWS + PAIR, :LANES])
        table_ref[PAIR * core : PAIR * core + PAIR] = rows.astype(jnp.int32)
    master[...] = update_state(mine_ref, theirs_ref, master_ref, moment1_ref, moment2_ref)[0]
    out_ref[...] = jnp.zeros_like(out_ref)
    for piece in range(PIECES):
        rows = master[PAIR * piece : PAIR * piece + PAIR, :]
        out_ref[position_ref[0, piece]] = rows.astype(jnp.bfloat16)


def step_states(position_ref, mine_ref, theirs_ref, master_ref, moment1_ref, moment2_ref, out_ref, state):
    fields = update_state(mine_ref, theirs_ref, master_ref, moment1_ref, moment2_ref)
    for index, field in enumerate(fields):
        state[index] = field * SCALES[index]
    out_ref[...] = jnp.zeros_like(out_ref)
    for piece in range(PIECES):
        place = position_ref[0, piece]
        for index in range(3):
            rows = state[index, PAIR * piece : PAIR * piece + PAIR, :]
            out_ref[place, :, WIDTH * index : WIDTH * (index + 1)] = rows


def place_states(slot_ref, arrived_ref, a_ref, b_ref, c_ref, placed):
    placed[...] = jnp.zeros_like(placed)
    for entry in range(DP * PAIR):
        placed[slot_ref[entry % 4, entry // 4]] = arrived_ref[entry]
    for index, ref in enumerate((a_ref, b_ref, c_ref)):
        rows = placed[:CAP, :, WIDTH * index : WIDTH * (index + 1)].reshape(PAIR * CAP, WIDTH)
        ref[...] = rows * (1.0 / SCALES[index])


def place_weights(slot_ref, arrived_ref, out_ref, placed):
    placed[...] = jnp.zeros_like(placed)
    for entry in range(DP * PAIR):
        placed[slot_ref[entry % 4, entry // 4]] = arrived_ref[entry].astype(jnp.float32)
    out_ref[...] = placed[:CAP].reshape(PAIR * CAP, WIDTH).astype(jnp.bfloat16)


def hold(value_ref, after_ref, out_ref):
    del value_ref, after_ref, out_ref


def f32(*shape):
    return jax.ShapeDtypeStruct(shape, jnp.float32)


def int32(*shape):
    return jax.ShapeDtypeStruct(shape, jnp.int32)


def bf16(*shape):
    return jax.ShapeDtypeStruct(shape, jnp.bfloat16)


def shards(activations, cotangent, master, first_moment, second_moment, new_owner, new_slot):
    dp_axes = ("z", "x", "c")
    core = lax.axis_index("c").astype(jnp.int32).reshape(1)
    packed, position = call(
        pack_cotangent, (bf16(CHIPS, 16, 2 * PAD), int32(1, LANES)), [SMEM] + [VMEM] * 3, (VMEM,) * 2, limit=WIDE_LIMIT
    )(core, new_owner.reshape(1, PIECES), new_slot.reshape(1, PIECES), cotangent)
    shared = lax.all_to_all(packed, ("z", "x"), split_axis=0, concat_axis=0, tiled=True)
    shared = shared.reshape(CHIPS * 16, 2 * PAD)

    act = lax.all_gather(activations, ("z", "x"), axis=0, tiled=True)

    right = [(i, (i + 1) % Y) for i in range(Y)]
    left = [(i, (i - 1) % Y) for i in range(Y)]
    down, up = [[shared[:PAD], shared[PAD:]]], [[shared[:PAD], shared[PAD:]]]
    for _ in range(Y // 2 - 1):
        down.append([lax.ppermute(half, "y", right) for half in down[-1]])
        up.append([lax.ppermute(half, "y", left) for half in up[-1]])
    far = [lax.ppermute(down[-1][0], "y", right), lax.ppermute(up[-1][1], "y", left)]
    parts = [shared] + [half for step in range(1, Y // 2) for way in (down, up) for half in way[step]] + far

    me = lax.axis_index("y").astype(jnp.int32).reshape(1)
    turned, turned_theirs, slots, slots_theirs = call(
        turn,
        (bf16(ROWS, Y * CHIPS * 16),) * 2 + (f32(8, LANES),) * 2,
        [SMEM] + [VMEM] * len(parts),
        (VMEM,) * 4,
        flops=1 << 28,
        scratch_shapes=[pltpu.VMEM((CHIPS, Y, 16, 2 * PAD), jnp.bfloat16)],
    )(me, *parts)
    theirs = call(theirs_grad, f32(ROWS + 8, WIDTH), [VMEM] * 3, VMEM, flops=1 << 31)(turned_theirs, act, slots_theirs)
    theirs = lax.ppermute(theirs, "c", [(0, 1), (1, 0)])
    mine = call(mine_grad, f32(ROWS, WIDTH), [VMEM] * 2, VMEM, flops=1 << 31)(turned, act)
    step = (position, mine, theirs, master, first_moment, second_moment)
    weights, slots = call(
        step_weights,
        (bf16(DP * PAIR, PAIR, WIDTH), int32(CORES * PAIR, LANES)),
        [SMEM] + [VMEM] * 5 + [SMEM, VMEM],
        (VMEM,) * 2,
        scratch_shapes=[pltpu.VMEM((ROWS, WIDTH), jnp.float32)],
    )(*step, core, slots)

    weights = lax.all_to_all(weights, dp_axes, split_axis=0, concat_axis=0, tiled=True)
    weights = call(
        place_weights,
        bf16(PAIR * CAP, WIDTH),
        [SMEM, VMEM],
        VMEM,
        scratch_shapes=[pltpu.VMEM((CAP + 1, PAIR, WIDTH), jnp.float32)],
    )(slots, weights)
    new_weights = lax.all_gather(weights, "y", axis=1, tiled=True)
    new_weights = call(
        copy_columns,
        bf16(*new_weights.shape),
        [ANY],
        ANY,
        limit=WIDE_LIMIT,
        scratch_shapes=[
            pltpu.VMEM((Y, PAIR * CAP, WIDTH), jnp.bfloat16),
            pltpu.SemaphoreType.DMA((Y,)),
            pltpu.SemaphoreType.DMA((Y,)),
        ],
    )(new_weights)

    states = call(
        step_states,
        f32(DP * PAIR, PAIR, 3 * WIDTH),
        [SMEM] + [VMEM] * 5,
        VMEM,
        flops=1 << 31,
        scratch_shapes=[pltpu.VMEM((3, ROWS, WIDTH), jnp.float32)],
    )(*step)
    states = call(hold, f32(*states.shape), [ANY, ANY], ANY, input_output_aliases={0: 0})(states, weights)
    states = states.astype(jnp.float16)
    arrived = lax.all_to_all(states, dp_axes, split_axis=0, concat_axis=0, tiled=True)
    placed = call(
        place_states,
        (f32(PAIR * CAP, WIDTH),) * 3,
        [SMEM, VMEM],
        (VMEM,) * 3,
        scratch_shapes=[pltpu.VMEM((CAP + 1, PAIR, 3 * WIDTH), jnp.float32)],
    )(slots, arrived.astype(jnp.float32))
    return (*placed, new_weights)


def solution(mesh):
    fine = Mesh(np.asarray(mesh.devices).reshape(Z, X, CORES, Y), ("z", "x", "c", "y"))
    dp = ("z", "x", "c")
    in_specs = (
        P(dp, "y"),
        P(dp + ("y",), None),
        P(dp, "y"),
        P(dp, "y"),
        P(dp, "y"),
        P(dp),
        P(dp),
    )
    out_specs = (P(dp, "y"), P(dp, "y"), P(dp, "y"), P(dp, None))
    return jax.shard_map(shards, mesh=fine, in_specs=in_specs, out_specs=out_specs, check_vma=False)
```

```python
import jax
import jax.numpy as jnp
import numpy as np
from jax import lax
from jax.experimental import pallas as pl
from jax.experimental.pallas import tpu as pltpu
from jax.sharding import Mesh, PartitionSpec as P

beta_one = 0.9
beta_two = 0.95
learn_rate = 0.1
adam_eps = 1e-08
adam_step = 1000
fix_one = 1.0 - beta_one**adam_step
fix_two = 1.0 - beta_two**adam_step

Z, X, CORES, Y = 8, 4, 2, 8
CHIPS = Z * X
DP = CHIPS * CORES
ROWS = 224
PAD = 256
PIECES = 112
PAIR = 2
CAP = 114
WIDTH = 512
LANES = 128
STRIPS = 4
STEPS = (0, -1, 1, -2, 2, -3, 3, 4)
SCALES = (1024.0, 64.0, 0.0625)

VMEM = pl.BlockSpec(memory_space=pltpu.VMEM)
SMEM = pl.BlockSpec(memory_space=pltpu.SMEM)
ANY = pl.BlockSpec(memory_space=pl.ANY)
LIMIT = 16 * 1024 * 1024
WIDE_LIMIT = 60 * 1024 * 1024


def call(kernel, out_shape, in_specs, out_specs, flops=0, limit=LIMIT, **kw):
    return pl.pallas_call(
        kernel,
        out_shape=out_shape,
        in_specs=in_specs,
        out_specs=out_specs,
        cost_estimate=pl.CostEstimate(flops=flops, bytes_accessed=4 << 20, transcendentals=0),
        compiler_params=pltpu.CompilerParams(vmem_limit_bytes=limit),
        **kw,
    )


def plan(owner_ref, slot_ref):
    shape = (LANES, LANES)

    def padded(ref):
        return jnp.concatenate([ref[...], jnp.full((1, LANES - PIECES), -1, jnp.int32)], axis=1)

    def column(row):
        return jnp.broadcast_to(row.astype(jnp.float32), shape).T.astype(jnp.int32)

    owner = padded(owner_ref)
    first, second = (lax.broadcasted_iota(jnp.int32, shape, dim) for dim in (0, 1))
    same = jnp.where((column(owner) == owner) & (first < second), 1, 0)
    rank = jnp.sum(same, axis=0, keepdims=True)
    lane = lax.broadcasted_iota(jnp.int32, (1, LANES), 1)
    position = jnp.where(lane < PIECES, owner * PAIR + rank, -1)
    found = jnp.where(column(position) == second, column(padded(slot_ref)) - CAP, 0)
    return position, jnp.sum(found, axis=0, keepdims=True) + CAP


def pack_cotangent(core_ref, owner_ref, slot_ref, cot_ref, out_ref, position_ref):
    position, slots = plan(owner_ref, slot_ref)
    position_ref[...] = position
    tokens = cot_ref.shape[0]
    slots = jnp.broadcast_to(slots.astype(jnp.float32), (tokens, LANES))
    spare = PAD - ROWS
    tail = lax.broadcasted_iota(jnp.int32, (tokens, LANES), 1) >= LANES - spare

    def fill(flip):
        for device in range(DP):
            start = ROWS * device
            entries = pltpu.roll(slots, (LANES - spare - PAIR * device) % LANES, 1)
            last = jnp.concatenate([cot_ref[:, start + LANES : start + ROWS], jnp.zeros((tokens, spare), jnp.bfloat16)], axis=1)
            last = jnp.where(tail, entries, last.astype(jnp.float32)).astype(jnp.bfloat16)
            place = PAD * ((device % CORES) ^ flip)
            out_ref[device // CORES, :, place : place + LANES] = cot_ref[:, start : start + LANES]
            out_ref[device // CORES, :, place + LANES : place + PAD] = last

    @pl.when(core_ref[0] == 0)
    def _():
        fill(0)

    @pl.when(core_ref[0] == 1)
    def _():
        fill(1)


def turn(me_ref, *refs):
    *parts, own_ref, other_ref, mine_ref, theirs_ref, tokens = refs
    half = Z // 2
    for number, ref in enumerate(parts):
        index = lax.rem(me_ref[0] + (Y + STEPS[(number + 1) // 2]), Y)
        count = ref.shape[0] // (X * 16)
        first = half * ((number + 1) % 2) if number else 0
        block = ref[...].reshape(count, X, 16, 2 * PAD)
        for z in range(count):
            tokens[:, first + z, index] = block[z]
    own_ref[...] = tokens[:, :, :, :, :PAD].reshape(CHIPS * Y * 16, PAD).T[:ROWS]
    other_ref[...] = tokens[:, :, :, :, PAD:].reshape(CHIPS * Y * 16, PAD).T[:ROWS]

    def received(start):
        tile = parts[0][:, start + LANES : start + PAD].astype(jnp.float32).reshape(CHIPS, 16, LANES)[:, 0]
        square = jnp.concatenate([tile, jnp.zeros((LANES - CHIPS, LANES), jnp.float32)], axis=0)
        return square.T[LANES - (PAD - ROWS) :][:8]

    mine_ref[...] = received(0)
    theirs_ref[...] = received(PAD)


def mine_grad(cot_ref, act_ref, out_ref):
    out_ref[...] = jnp.dot(cot_ref[...], act_ref[...], preferred_element_type=jnp.float32)


def theirs_grad(cot_ref, act_ref, slots_ref, out_ref):
    out_ref[:ROWS] = jnp.dot(cot_ref[...], act_ref[...], preferred_element_type=jnp.float32)
    out_ref[ROWS:, :LANES] = slots_ref[...]
    out_ref[ROWS:, LANES:] = jnp.zeros((8, WIDTH - LANES), jnp.float32)


def copy_columns(in_ref, out_ref, held, in_sem, out_sem):
    copies = []
    for part in range(STRIPS):
        width = in_ref.shape[1] // STRIPS
        columns = pl.ds(width * part, width)
        copies.append(
            (
                pltpu.make_async_copy(in_ref.at[:, columns], held.at[part], in_sem.at[part]),
                pltpu.make_async_copy(held.at[part], out_ref.at[:, columns], out_sem.at[part]),
            )
        )
    for arrive, _ in copies:
        arrive.start()
    for arrive, leave in copies:
        arrive.wait()
        leave.start()
    for _, leave in copies:
        leave.wait()


def update_state(mine_ref, theirs_ref, master_ref, moment1_ref, moment2_ref):
    grad = mine_ref[...] + theirs_ref[:ROWS]
    moment1 = beta_one * moment1_ref[...] + (1.0 - beta_one) * grad
    moment2 = beta_two * moment2_ref[...] + (1.0 - beta_two) * grad * grad
    update = learn_rate * (moment1 / fix_one) / (jnp.sqrt(moment2 / fix_two) + adam_eps)
    return master_ref[...] - update, moment1, moment2


def step_weights(
    position_ref, mine_ref, theirs_ref, master_ref, moment1_ref, moment2_ref, core_ref, slots_ref, out_ref, table_ref, master
):
    for core in range(CORES):
        rows = jnp.where(core_ref[0] == core, slots_ref[:PAIR], theirs_ref[ROWS : ROWS + PAIR, :LANES])
        table_ref[PAIR * core : PAIR * core + PAIR] = rows.astype(jnp.int32)
    master[...] = update_state(mine_ref, theirs_ref, master_ref, moment1_ref, moment2_ref)[0]
    out_ref[...] = jnp.zeros_like(out_ref)
    for piece in range(PIECES):
        rows = master[PAIR * piece : PAIR * piece + PAIR, :]
        out_ref[position_ref[0, piece]] = rows.astype(jnp.bfloat16)


def step_states(position_ref, mine_ref, theirs_ref, master_ref, moment1_ref, moment2_ref, out_ref, state):
    fields = update_state(mine_ref, theirs_ref, master_ref, moment1_ref, moment2_ref)
    for index, field in enumerate(fields):
        state[index] = field * SCALES[index]
    out_ref[...] = jnp.zeros_like(out_ref)
    for piece in range(PIECES):
        place = position_ref[0, piece]
        for index in range(3):
            rows = state[index, PAIR * piece : PAIR * piece + PAIR, :]
            out_ref[place, :, WIDTH * index : WIDTH * (index + 1)] = rows


def place_states(slot_ref, arrived_ref, a_ref, b_ref, c_ref, placed):
    placed[...] = jnp.zeros_like(placed)
    for entry in range(DP * PAIR):
        placed[slot_ref[entry % 4, entry // 4]] = arrived_ref[entry]
    for index, ref in enumerate((a_ref, b_ref, c_ref)):
        rows = placed[:CAP, :, WIDTH * index : WIDTH * (index + 1)].reshape(PAIR * CAP, WIDTH)
        ref[...] = rows * (1.0 / SCALES[index])


def place_weights(slot_ref, arrived_ref, out_ref, placed):
    placed[...] = jnp.zeros_like(placed)
    for entry in range(DP * PAIR):
        placed[slot_ref[entry % 4, entry // 4]] = arrived_ref[entry].astype(jnp.float32)
    out_ref[...] = placed[:CAP].reshape(PAIR * CAP, WIDTH).astype(jnp.bfloat16)


def hold(value_ref, after_ref, out_ref):
    del value_ref, after_ref, out_ref


def f32(*shape):
    return jax.ShapeDtypeStruct(shape, jnp.float32)


def int32(*shape):
    return jax.ShapeDtypeStruct(shape, jnp.int32)


def bf16(*shape):
    return jax.ShapeDtypeStruct(shape, jnp.bfloat16)


def shards(activations, cotangent, master, first_moment, second_moment, new_owner, new_slot):
    dp_axes = ("z", "x", "c")
    core = lax.axis_index("c").astype(jnp.int32).reshape(1)
    packed, position = call(
        pack_cotangent, (bf16(CHIPS, 16, 2 * PAD), int32(1, LANES)), [SMEM] + [VMEM] * 3, (VMEM,) * 2, limit=WIDE_LIMIT
    )(core, new_owner.reshape(1, PIECES), new_slot.reshape(1, PIECES), cotangent)
    shared = lax.all_to_all(packed, ("z", "x"), split_axis=0, concat_axis=0, tiled=True)
    shared = shared.reshape(CHIPS * 16, 2 * PAD)

    act = lax.all_gather(activations, ("x", "z"), axis=0, tiled=True)

    right = [(i, (i + 1) % Y) for i in range(Y)]
    left = [(i, (i - 1) % Y) for i in range(Y)]
    down, up = [[shared[:PAD], shared[PAD:]]], [[shared[:PAD], shared[PAD:]]]
    for _ in range(Y // 2 - 1):
        down.append([lax.ppermute(half, "y", right) for half in down[-1]])
        up.append([lax.ppermute(half, "y", left) for half in up[-1]])
    far = [lax.ppermute(down[-1][0], "y", right), lax.ppermute(up[-1][1], "y", left)]
    parts = [shared] + [half for step in range(1, Y // 2) for way in (down, up) for half in way[step]] + far

    me = lax.axis_index("y").astype(jnp.int32).reshape(1)
    turned, turned_theirs, slots, slots_theirs = call(
        turn,
        (bf16(ROWS, Y * CHIPS * 16),) * 2 + (f32(8, LANES),) * 2,
        [SMEM] + [VMEM] * len(parts),
        (VMEM,) * 4,
        flops=1 << 28,
        scratch_shapes=[pltpu.VMEM((X, Z, Y, 16, 2 * PAD), jnp.bfloat16)],
    )(me, *parts)
    theirs = call(theirs_grad, f32(ROWS + 8, WIDTH), [VMEM] * 3, VMEM, flops=1 << 31)(turned_theirs, act, slots_theirs)
    theirs = lax.ppermute(theirs, "c", [(0, 1), (1, 0)])
    mine = call(mine_grad, f32(ROWS, WIDTH), [VMEM] * 2, VMEM, flops=1 << 31)(turned, act)
    step = (position, mine, theirs, master, first_moment, second_moment)
    weights, slots = call(
        step_weights,
        (bf16(DP * PAIR, PAIR, WIDTH), int32(CORES * PAIR, LANES)),
        [SMEM] + [VMEM] * 5 + [SMEM, VMEM],
        (VMEM,) * 2,
        scratch_shapes=[pltpu.VMEM((ROWS, WIDTH), jnp.float32)],
    )(*step, core, slots)

    weights = lax.all_to_all(weights, dp_axes, split_axis=0, concat_axis=0, tiled=True)
    weights = call(
        place_weights,
        bf16(PAIR * CAP, WIDTH),
        [SMEM, VMEM],
        VMEM,
        scratch_shapes=[pltpu.VMEM((CAP + 1, PAIR, WIDTH), jnp.float32)],
    )(slots, weights)
    new_weights = lax.all_gather(weights, "y", axis=1, tiled=True)
    new_weights = call(
        copy_columns,
        bf16(*new_weights.shape),
        [ANY],
        ANY,
        limit=WIDE_LIMIT,
        scratch_shapes=[
            pltpu.VMEM((STRIPS, PAIR * CAP, Y * WIDTH // STRIPS), jnp.bfloat16),
            pltpu.SemaphoreType.DMA((STRIPS,)),
            pltpu.SemaphoreType.DMA((STRIPS,)),
        ],
    )(new_weights)

    states = call(
        step_states,
        f32(DP * PAIR, PAIR, 3 * WIDTH),
        [SMEM] + [VMEM] * 5,
        VMEM,
        flops=1 << 31,
        scratch_shapes=[pltpu.VMEM((3, ROWS, WIDTH), jnp.float32)],
    )(*step)
    states = call(hold, f32(*states.shape), [ANY, ANY], ANY, input_output_aliases={0: 0})(states, weights)
    states = states.astype(jnp.float16)
    arrived = lax.all_to_all(states, dp_axes, split_axis=0, concat_axis=0, tiled=True)
    placed = call(
        place_states,
        (f32(PAIR * CAP, WIDTH),) * 3,
        [SMEM, VMEM],
        (VMEM,) * 3,
        scratch_shapes=[pltpu.VMEM((CAP + 1, PAIR, 3 * WIDTH), jnp.float32)],
    )(slots, arrived.astype(jnp.float32))
    return (*placed, new_weights)


def solution(mesh):
    fine = Mesh(np.asarray(mesh.devices).reshape(Z, X, CORES, Y), ("z", "x", "c", "y"))
    dp = ("z", "x", "c")
    in_specs = (
        P(dp, "y"),
        P(dp + ("y",), None),
        P(dp, "y"),
        P(dp, "y"),
        P(dp, "y"),
        P(dp),
        P(dp),
    )
    out_specs = (P(dp, "y"), P(dp, "y"), P(dp, "y"), P(dp, None))
    return jax.shard_map(shards, mesh=fine, in_specs=in_specs, out_specs=out_specs, check_vma=False)
```

```python
import jax
import jax.numpy as jnp
import numpy as np
from jax import lax
from jax.experimental import pallas as pl
from jax.experimental.pallas import tpu as pltpu
from jax.sharding import Mesh, PartitionSpec as P

beta_one = 0.9
beta_two = 0.95
learn_rate = 0.1
adam_eps = 1e-08
adam_step = 1000
fix_one = 1.0 - beta_one**adam_step
fix_two = 1.0 - beta_two**adam_step

Z, X, CORES, Y = 8, 4, 2, 8
CHIPS = Z * X
DP = CHIPS * CORES
ROWS = 224
PAD = 256
PIECES = 112
PAIR = 2
CAP = 114
WIDTH = 512
LANES = 128
STRIPS = 4
STEPS = (0, -1, 1, -2, 2, -3, 3, 4)
SCALES = (1024.0, 64.0, 0.0625)

VMEM = pl.BlockSpec(memory_space=pltpu.VMEM)
SMEM = pl.BlockSpec(memory_space=pltpu.SMEM)
ANY = pl.BlockSpec(memory_space=pl.ANY)
LIMIT = 16 * 1024 * 1024
WIDE_LIMIT = 60 * 1024 * 1024


def call(kernel, out_shape, in_specs, out_specs, flops=0, limit=LIMIT, **kw):
    return pl.pallas_call(
        kernel,
        out_shape=out_shape,
        in_specs=in_specs,
        out_specs=out_specs,
        cost_estimate=pl.CostEstimate(flops=flops, bytes_accessed=4 << 20, transcendentals=0),
        compiler_params=pltpu.CompilerParams(vmem_limit_bytes=limit),
        **kw,
    )


def plan(owner_ref, slot_ref):
    shape = (LANES, LANES)

    def padded(ref):
        return jnp.concatenate([ref[...], jnp.full((1, LANES - PIECES), -1, jnp.int32)], axis=1)

    def column(row):
        return jnp.broadcast_to(row.astype(jnp.float32), shape).T.astype(jnp.int32)

    owner = padded(owner_ref)
    first, second = (lax.broadcasted_iota(jnp.int32, shape, dim) for dim in (0, 1))
    same = jnp.where((column(owner) == owner) & (first < second), 1, 0)
    rank = jnp.sum(same, axis=0, keepdims=True)
    lane = lax.broadcasted_iota(jnp.int32, (1, LANES), 1)
    position = jnp.where(lane < PIECES, owner * PAIR + rank, -1)
    found = jnp.where(column(position) == second, column(padded(slot_ref)) - CAP, 0)
    return position, jnp.sum(found, axis=0, keepdims=True) + CAP


def pack_cotangent(core_ref, owner_ref, slot_ref, cot_ref, out_ref, position_ref):
    position, slots = plan(owner_ref, slot_ref)
    position_ref[...] = position
    tokens = cot_ref.shape[0]
    slots = jnp.broadcast_to(slots.astype(jnp.float32), (tokens, LANES))
    spare = PAD - ROWS
    tail = lax.broadcasted_iota(jnp.int32, (tokens, LANES), 1) >= LANES - spare

    def fill(flip):
        for device in range(DP):
            start = ROWS * device
            entries = pltpu.roll(slots, (LANES - spare - PAIR * device) % LANES, 1)
            last = jnp.concatenate([cot_ref[:, start + LANES : start + ROWS], jnp.zeros((tokens, spare), jnp.bfloat16)], axis=1)
            last = jnp.where(tail, entries, last.astype(jnp.float32)).astype(jnp.bfloat16)
            place = PAD * ((device % CORES) ^ flip)
            out_ref[device // CORES, :, place : place + LANES] = cot_ref[:, start : start + LANES]
            out_ref[device // CORES, :, place + LANES : place + PAD] = last

    @pl.when(core_ref[0] == 0)
    def _():
        fill(0)

    @pl.when(core_ref[0] == 1)
    def _():
        fill(1)


def turn(me_ref, *refs):
    *parts, own_ref, other_ref, mine_ref, theirs_ref, tokens = refs
    half = Z // 2
    for number, ref in enumerate(parts):
        index = lax.rem(me_ref[0] + (Y + STEPS[(number + 1) // 2]), Y)
        count = ref.shape[0] // (X * 16)
        first = half * ((number + 1) % 2) if number else 0
        block = ref[...].reshape(count, X, 16, 2 * PAD)
        for z in range(count):
            tokens[:, first + z, index] = block[z]
    own_ref[...] = tokens[:, :, :, :, :PAD].reshape(CHIPS * Y * 16, PAD).T[:ROWS]
    other_ref[...] = tokens[:, :, :, :, PAD:].reshape(CHIPS * Y * 16, PAD).T[:ROWS]

    def received(start):
        tile = parts[0][:, start + LANES : start + PAD].astype(jnp.float32).reshape(CHIPS, 16, LANES)[:, 0]
        square = jnp.concatenate([tile, jnp.zeros((LANES - CHIPS, LANES), jnp.float32)], axis=0)
        return square.T[LANES - (PAD - ROWS) :][:8]

    mine_ref[...] = received(0)
    theirs_ref[...] = received(PAD)


def mine_grad(cot_ref, act_ref, out_ref):
    out_ref[...] = jnp.dot(cot_ref[...], act_ref[...], preferred_element_type=jnp.float32)


def theirs_grad(cot_ref, act_ref, slots_ref, out_ref):
    out_ref[:ROWS] = jnp.dot(cot_ref[...], act_ref[...], preferred_element_type=jnp.float32)
    out_ref[ROWS:, :LANES] = slots_ref[...]
    out_ref[ROWS:, LANES:] = jnp.zeros((8, WIDTH - LANES), jnp.float32)


def copy_columns(in_ref, out_ref, held, in_sem, out_sem):
    copies = []
    for part in range(STRIPS):
        width = in_ref.shape[1] // STRIPS
        columns = pl.ds(width * part, width)
        copies.append(
            (
                pltpu.make_async_copy(in_ref.at[:, columns], held.at[part], in_sem.at[part]),
                pltpu.make_async_copy(held.at[part], out_ref.at[:, columns], out_sem.at[part]),
            )
        )
    for arrive, _ in copies:
        arrive.start()
    for arrive, leave in copies:
        arrive.wait()
        leave.start()
    for _, leave in copies:
        leave.wait()


def update_state(mine_ref, theirs_ref, master_ref, moment1_ref, moment2_ref):
    grad = mine_ref[...] + theirs_ref[:ROWS]
    moment1 = beta_one * moment1_ref[...] + (1.0 - beta_one) * grad
    moment2 = beta_two * moment2_ref[...] + (1.0 - beta_two) * grad * grad
    update = learn_rate * (moment1 / fix_one) / (jnp.sqrt(moment2 / fix_two) + adam_eps)
    return master_ref[...] - update, moment1, moment2


def step_weights(
    position_ref, mine_ref, theirs_ref, master_ref, moment1_ref, moment2_ref, core_ref, slots_ref, out_ref, table_ref, master
):
    for core in range(CORES):
        rows = jnp.where(core_ref[0] == core, slots_ref[:PAIR], theirs_ref[ROWS : ROWS + PAIR, :LANES])
        table_ref[PAIR * core : PAIR * core + PAIR] = rows.astype(jnp.int32)
    master[...] = update_state(mine_ref, theirs_ref, master_ref, moment1_ref, moment2_ref)[0]
    out_ref[...] = jnp.zeros_like(out_ref)
    for piece in range(PIECES):
        rows = master[PAIR * piece : PAIR * piece + PAIR, :]
        out_ref[position_ref[0, piece]] = rows.astype(jnp.bfloat16)


def step_states(position_ref, mine_ref, theirs_ref, master_ref, moment1_ref, moment2_ref, out_ref, state):
    fields = update_state(mine_ref, theirs_ref, master_ref, moment1_ref, moment2_ref)
    for index, field in enumerate(fields):
        state[index] = field * SCALES[index]
    out_ref[...] = jnp.zeros_like(out_ref)
    for piece in range(PIECES):
        place = position_ref[0, piece]
        for index in range(3):
            rows = state[index, PAIR * piece : PAIR * piece + PAIR, :]
            out_ref[place, :, WIDTH * index : WIDTH * (index + 1)] = rows


def place_states(slot_ref, arrived_ref, a_ref, b_ref, c_ref, placed):
    placed[...] = jnp.zeros_like(placed)
    for entry in range(DP * PAIR):
        placed[slot_ref[entry % 4, entry // 4]] = arrived_ref[entry]
    for index, ref in enumerate((a_ref, b_ref, c_ref)):
        rows = placed[:CAP, :, WIDTH * index : WIDTH * (index + 1)].reshape(PAIR * CAP, WIDTH)
        ref[...] = rows * (1.0 / SCALES[index])


def place_weights(slot_ref, arrived_ref, out_ref, placed):
    placed[...] = jnp.zeros_like(placed)
    for entry in range(DP * PAIR):
        placed[slot_ref[entry % 4, entry // 4]] = arrived_ref[entry].astype(jnp.float32)
    out_ref[...] = placed[:CAP].reshape(PAIR * CAP, WIDTH).astype(jnp.bfloat16)


def hold_index(value_ref, after_ref, out_ref):
    del after_ref
    out_ref[0] = value_ref[0]


def hold(value_ref, after_ref, out_ref):
    del value_ref, after_ref, out_ref


def f32(*shape):
    return jax.ShapeDtypeStruct(shape, jnp.float32)


def int32(*shape):
    return jax.ShapeDtypeStruct(shape, jnp.int32)


def bf16(*shape):
    return jax.ShapeDtypeStruct(shape, jnp.bfloat16)


def shards(activations, cotangent, master, first_moment, second_moment, new_owner, new_slot):
    dp_axes = ("z", "x", "c")
    core = lax.axis_index("c").astype(jnp.int32).reshape(1)
    packed, position = call(
        pack_cotangent, (bf16(CHIPS, 16, 2 * PAD), int32(1, LANES)), [SMEM] + [VMEM] * 3, (VMEM,) * 2, limit=WIDE_LIMIT
    )(core, new_owner.reshape(1, PIECES), new_slot.reshape(1, PIECES), cotangent)
    shared = lax.all_to_all(packed, ("z", "x"), split_axis=0, concat_axis=0, tiled=True)
    shared = shared.reshape(CHIPS * 16, 2 * PAD)

    act = lax.all_gather(activations, ("x", "z"), axis=0, tiled=True)

    right = [(i, (i + 1) % Y) for i in range(Y)]
    left = [(i, (i - 1) % Y) for i in range(Y)]
    down, up = [[shared[:PAD], shared[PAD:]]], [[shared[:PAD], shared[PAD:]]]
    for _ in range(Y // 2 - 1):
        down.append([lax.ppermute(half, "y", right) for half in down[-1]])
        up.append([lax.ppermute(half, "y", left) for half in up[-1]])
    far = [lax.ppermute(down[-1][0], "y", right), lax.ppermute(up[-1][1], "y", left)]
    parts = [shared] + [half for step in range(1, Y // 2) for way in (down, up) for half in way[step]] + far

    me = lax.axis_index("y").astype(jnp.int32).reshape(1)
    me = call(hold_index, int32(1), [SMEM, ANY], SMEM, limit=WIDE_LIMIT)(me, act)
    turned, turned_theirs, slots, slots_theirs = call(
        turn,
        (bf16(ROWS, Y * CHIPS * 16),) * 2 + (f32(8, LANES),) * 2,
        [SMEM] + [VMEM] * len(parts),
        (VMEM,) * 4,
        flops=1 << 28,
        scratch_shapes=[pltpu.VMEM((X, Z, Y, 16, 2 * PAD), jnp.bfloat16)],
    )(me, *parts)
    theirs = call(theirs_grad, f32(ROWS + 8, WIDTH), [VMEM] * 3, VMEM, flops=1 << 31)(turned_theirs, act, slots_theirs)
    theirs = lax.ppermute(theirs, "c", [(0, 1), (1, 0)])
    mine = call(mine_grad, f32(ROWS, WIDTH), [VMEM] * 2, VMEM, flops=1 << 31)(turned, act)
    step = (position, mine, theirs, master, first_moment, second_moment)
    weights, slots = call(
        step_weights,
        (bf16(DP * PAIR, PAIR, WIDTH), int32(CORES * PAIR, LANES)),
        [SMEM] + [VMEM] * 5 + [SMEM, VMEM],
        (VMEM,) * 2,
        scratch_shapes=[pltpu.VMEM((ROWS, WIDTH), jnp.float32)],
    )(*step, core, slots)

    weights = lax.all_to_all(weights, dp_axes, split_axis=0, concat_axis=0, tiled=True)
    weights = call(
        place_weights,
        bf16(PAIR * CAP, WIDTH),
        [SMEM, VMEM],
        VMEM,
        scratch_shapes=[pltpu.VMEM((CAP + 1, PAIR, WIDTH), jnp.float32)],
    )(slots, weights)
    new_weights = lax.all_gather(weights, "y", axis=1, tiled=True)
    new_weights = call(
        copy_columns,
        bf16(*new_weights.shape),
        [ANY],
        ANY,
        limit=WIDE_LIMIT,
        scratch_shapes=[
            pltpu.VMEM((STRIPS, PAIR * CAP, Y * WIDTH // STRIPS), jnp.bfloat16),
            pltpu.SemaphoreType.DMA((STRIPS,)),
            pltpu.SemaphoreType.DMA((STRIPS,)),
        ],
    )(new_weights)

    states = call(
        step_states,
        f32(DP * PAIR, PAIR, 3 * WIDTH),
        [SMEM] + [VMEM] * 5,
        VMEM,
        flops=1 << 31,
        scratch_shapes=[pltpu.VMEM((3, ROWS, WIDTH), jnp.float32)],
    )(*step)
    states = call(hold, f32(*states.shape), [ANY, ANY], ANY, input_output_aliases={0: 0})(states, weights)
    states = states.astype(jnp.float16)
    arrived = lax.all_to_all(states, dp_axes, split_axis=0, concat_axis=0, tiled=True)
    placed = call(
        place_states,
        (f32(PAIR * CAP, WIDTH),) * 3,
        [SMEM, VMEM],
        (VMEM,) * 3,
        scratch_shapes=[pltpu.VMEM((CAP + 1, PAIR, 3 * WIDTH), jnp.float32)],
    )(slots, arrived.astype(jnp.float32))
    return (*placed, new_weights)


def solution(mesh):
    fine = Mesh(np.asarray(mesh.devices).reshape(Z, X, CORES, Y), ("z", "x", "c", "y"))
    dp = ("z", "x", "c")
    in_specs = (
        P(dp, "y"),
        P(dp + ("y",), None),
        P(dp, "y"),
        P(dp, "y"),
        P(dp, "y"),
        P(dp),
        P(dp),
    )
    out_specs = (P(dp, "y"), P(dp, "y"), P(dp, "y"), P(dp, None))
    return jax.shard_map(shards, mesh=fine, in_specs=in_specs, out_specs=out_specs, check_vma=False)
```
